512 devices in a mesh: clip: 32 (over z, core), frame: 16 (over x, y).
Axes of the slice: x: 4, y: 4, z: 16, core: 2. Of those that a mesh axis runs over, the one named last changes fastest.
Arguments:
- inputs: bfloat16 [32, 5, 128, 64, 128], P('clip', None, 'frame'), may hold values from -16 to 16
- norm_gain: float32 [128], replicated, may hold values from 0.1 to 1.9
- norm_bias: float32 [128], replicated, may hold values from -3 to 3
- conv_weight: bfloat16 [3, 3, 3, 128, 128], replicated, may hold values from -0.109375 to 0.109375
- conv_bias: float32 [128], replicated, may hold values from -3 to 3
- down_weight: bfloat16 [3, 3, 128, 128], replicated, may hold values from -0.1875 to 0.1875
- down_bias: float32 [128], replicated, may hold values from -3 to 3
- time_weight: bfloat16 [3, 128, 128], replicated, may hold values from -0.3125 to 0.3125
- time_bias: float32 [128], replicated, may hold values from -3 to 3
- head_weight: bfloat16 [128, 32], replicated, may hold values from -0.5 to 0.5
- head_bias: float32 [32], replicated, may hold values from -3 to 3
- tile_shard: int32 [32, 3, 512], P('clip', None, 'frame'), may hold values from 0 to 31, as said below
- tile_slot: int32 [32, 3, 512], P('clip', None, 'frame'), may hold values from 0 to 1023, as said below
Outputs:
- packed: bfloat16 [3, 32768, 128], P(None, ('clip', 'frame'))
The draws below stay inside these ranges and needn't reach their ends.
Inputs may be any that keep to these rules, and one draw needn't show every extreme that they name: `tile_shard`: tiles t of one clip and reduced frame with t // 32 = g form block g. In every such block at most 2 tiles go to one shard, and in every reduced frame and block some shard receives exactly 2 tiles from every clip. `tile_slot`: the tiles of block g sent to one shard in one reduced frame have distinct slots from g * 64 to (g + 1) * 64 - 1.
All inputs are finite; a program needn't handle non-finite values.
Results may differ from the reference program's by a relative error of at most 0.006.
Values may be sent and summed in bfloat16 or wider, within the bound.
No kernel may reach another device: no remote copies, remote signals or barrier semaphores. Data moves between devices by JAX's collectives and lax.ppermute only.
A program may use at most 64 MiB of HBM per device.

```python
import jax
import jax.numpy as jnp
from jax import lax

CH = 128
ZCH = 32
GROUPS = 32
FRAMES = 5
COLS = 64
ROWS = 128
CLIPS = 32
LAT_FRAMES = 3
TILES_DEV = 32
TILES = 512
BASE = 1
SLOTS = 64
CAP = 1024


def draw_inputs(key, part):
    noise_key = jax.random.fold_in(key, 0)
    chan_key = jax.random.fold_in(key, 1)
    amp_key = jax.random.fold_in(key, 4)
    sign_key = jax.random.fold_in(key, 5)
    shape_all = (CLIPS, FRAMES, ROWS, COLS, CH)
    row_pos = jnp.arange(ROWS, dtype=jnp.float32) / max(ROWS - 1, 1)
    rising = (0.6 * jnp.exp(row_pos * jnp.log(3.0)))[None, None, :, None, None]
    chan_scale = jnp.exp(jax.random.uniform(chan_key, (CH,), jnp.float32, jnp.log(0.5), jnp.log(2.0)))
    chan_sign = jnp.where(jax.random.uniform(sign_key, (CH,), jnp.float32) < 0.5, -1.0, 1.0)
    chan_amp = jax.random.uniform(amp_key, (CH,), jnp.float32, 0.6, 1.4) * chan_sign
    mean_ramp = (0.5 * jnp.exp(row_pos * jnp.log(3.0)))[None, None, :, None, None]
    values = jax.random.normal(noise_key, shape_all, jnp.float32) * rising * chan_scale + mean_ramp * chan_amp
    return jnp.clip(values, -16.0, 16.0).astype(jnp.bfloat16)


def packing_lists(key):
    base_key = jax.random.fold_in(key, 11)
    blocks = TILES // TILES_DEV

    def one_block(block_key, block_id):
        order_key, moves_key, slot_key, shuffle_key = jax.random.split(block_key, 4)
        shard_order = jax.random.permutation(order_key, CLIPS)
        pair_count = CLIPS // 2
        shifts_by = jax.random.randint(moves_key, (CLIPS, pair_count), 0, BASE + 1)
        shifts_by = shifts_by.at[:, 0].set(BASE)
        richer = shard_order[0::2]
        poorer = shard_order[1::2]
        counts = jnp.zeros((CLIPS, CLIPS), jnp.int32)
        counts = counts.at[:, richer].set(BASE + shifts_by).at[:, poorer].set(BASE - shifts_by)
        run_ends = jnp.cumsum(counts, axis=1)
        run_starts = run_ends - counts
        tile_pos = jnp.arange(TILES_DEV, dtype=jnp.int32)
        shard_sorted = jnp.sum((run_ends[:, None, :] <= tile_pos[None, :, None]).astype(jnp.int32), axis=2)
        rank_sorted = tile_pos[None, :] - jnp.take_along_axis(run_starts, shard_sorted, axis=1)
        before = jnp.cumsum(counts, axis=0) - counts
        position = jnp.take_along_axis(before, shard_sorted, axis=1) + rank_sorted
        slot_perm = jax.vmap(lambda sub_key: jax.random.permutation(sub_key, SLOTS))(jax.random.split(slot_key, CLIPS))
        slot_sorted = slot_perm[shard_sorted, position] + block_id * SLOTS
        shuffle = jax.vmap(lambda sub_key: jax.random.permutation(sub_key, TILES_DEV))(jax.random.split(shuffle_key, CLIPS))
        dest_ids = jnp.take_along_axis(shard_sorted, shuffle, axis=1)
        slot_ids = jnp.take_along_axis(slot_sorted, shuffle, axis=1)
        return (dest_ids.astype(jnp.int32), slot_ids.astype(jnp.int32))
    block_ids = jnp.arange(LAT_FRAMES * blocks, dtype=jnp.int32) % blocks
    dest_ids, slot_ids = jax.vmap(one_block)(jax.random.split(base_key, LAT_FRAMES * blocks), block_ids)
    dest_ids = dest_ids.reshape(LAT_FRAMES, blocks, CLIPS, TILES_DEV).transpose(2, 0, 1, 3).reshape(CLIPS, LAT_FRAMES, TILES)
    slot_ids = slot_ids.reshape(LAT_FRAMES, blocks, CLIPS, TILES_DEV).transpose(2, 0, 1, 3).reshape(CLIPS, LAT_FRAMES, TILES)
    return (dest_ids, slot_ids)


def draw_tile_shard(key, part):
    return packing_lists(key)[0]


def draw_tile_slot(key, part):
    return packing_lists(key)[1]


def gaussian(own_key, dims, width, most, kind=jnp.bfloat16):
    values = width * jax.random.normal(own_key, dims, jnp.float32)
    return jnp.clip(values, min=-most, max=most).astype(kind)


def setup_inputs(seed: int = 0) -> dict:
    arg_keys = jax.random.split(jax.random.key(seed), 14)
    return {
        "inputs": draw_inputs(jax.random.fold_in(arg_keys[13], 71), 0),
        "norm_gain": jnp.clip(1.0 + 0.18 * jax.random.normal(arg_keys[1], (CH,), jnp.float32), 0.1, 1.9),
        "norm_bias": gaussian(arg_keys[2], (CH,), 0.5, 3.0, jnp.float32),
        "conv_weight": gaussian(arg_keys[3], (3, 3, 3, CH, CH), (27 * CH) ** -0.5, 0.109375),
        "conv_bias": gaussian(arg_keys[4], (CH,), 0.5, 3.0, jnp.float32),
        "down_weight": gaussian(arg_keys[5], (3, 3, CH, CH), (9 * CH) ** -0.5, 0.1875),
        "down_bias": gaussian(arg_keys[6], (CH,), 0.5, 3.0, jnp.float32),
        "time_weight": gaussian(arg_keys[7], (3, CH, CH), (3 * CH) ** -0.5, 0.3125),
        "time_bias": gaussian(arg_keys[8], (CH,), 0.5, 3.0, jnp.float32),
        "head_weight": gaussian(arg_keys[9], (CH, ZCH), CH ** -0.5, 0.5),
        "head_bias": gaussian(arg_keys[10], (ZCH,), 0.5, 3.0, jnp.float32),
        "tile_shard": draw_tile_shard(jax.random.fold_in(arg_keys[13], 71), 0),
        "tile_slot": draw_tile_slot(jax.random.fold_in(arg_keys[13], 71), 0),
    }


EPSILON = 1e-06

def causal_mix(stacked_pad, weight, bias_vec, frame_count, row_count, col_count):
    channels = weight.shape[-1]
    col_stack = jnp.concatenate([stacked_pad[:, :, col_tap:col_tap + col_count] for col_tap in range(3)], axis=-1)
    accum_sum = jnp.zeros((frame_count * row_count * col_count, channels), jnp.float32)
    for time_tap in range(3):
        for row_tap in range(3):
            stacked = col_stack[time_tap:time_tap + frame_count, row_tap:row_tap + row_count]
            accum_sum = accum_sum + jnp.dot(stacked.reshape(-1, 3 * channels), weight[time_tap, row_tap].reshape(3 * channels, channels), preferred_element_type=jnp.float32)
    return accum_sum.reshape(frame_count, row_count, col_count, channels) + bias_vec

def strided_mix(padded, weight, bias_vec, row_out, col_out):
    frame_count = padded.shape[0]
    channels = weight.shape[-1]
    accum_sum = jnp.zeros((frame_count * row_out * col_out, channels), jnp.float32)
    for row_tap in range(3):
        window = padded[:, row_tap:row_tap + 2 * row_out:2]
        stacked = jnp.concatenate([window[:, :, col_tap:col_tap + 2 * col_out:2] for col_tap in range(3)], axis=-1)
        accum_sum = accum_sum + jnp.dot(stacked.reshape(-1, 3 * channels), weight[row_tap].reshape(3 * channels, channels), preferred_element_type=jnp.float32)
    return accum_sum.reshape(frame_count, row_out, col_out, channels) + bias_vec

def time_mix(padded, weight, bias_vec, lat_count):
    channels = weight.shape[-1]
    rest = padded.shape[1:3]
    accum_sum = jnp.zeros((lat_count * rest[0] * rest[1], channels), jnp.float32)
    for time_tap in range(3):
        window = padded[time_tap:time_tap + 2 * lat_count - 1:2]
        accum_sum = accum_sum + jnp.dot(window.reshape(-1, channels), weight[time_tap], preferred_element_type=jnp.float32)
    return accum_sum.reshape(lat_count, rest[0], rest[1], channels) + bias_vec

def project_head(lat_mixed, head_weight, head_bias):
    lat_count, row_count, col_count, channels = lat_mixed.shape
    out_channels = head_weight.shape[1]
    latent = jnp.dot(lat_mixed.reshape(-1, channels), head_weight, preferred_element_type=jnp.float32) + head_bias
    return latent.astype(jnp.bfloat16).reshape(lat_count, row_count, col_count, out_channels)

def to_tiles(latent):
    lat_count, row_count, col_count, out_channels = latent.shape
    split_up = latent.reshape(lat_count, row_count // 2, 2, col_count // 2, 2, out_channels)
    split_up = split_up.transpose(0, 1, 3, 2, 4, 5)
    return split_up.reshape(lat_count, row_count // 2 * (col_count // 2), 4 * out_channels)

def reference(inputs, norm_gain, norm_bias, conv_weight, conv_bias, down_weight, down_bias, time_weight, time_bias, head_weight, head_bias, tile_shard, tile_slot):

    def encode_clip(clip_data):
        grouped = clip_data.astype(jnp.float32).reshape(FRAMES, ROWS, COLS, GROUPS, CH // GROUPS)
        group_mean = lax.optimization_barrier(jnp.mean(grouped, axis=(0, 1, 2, 4)))
        centred = grouped - group_mean[:, None]
        group_var = lax.optimization_barrier(jnp.mean(centred * centred, axis=(0, 1, 2, 4)))
        normed = (centred * lax.rsqrt(group_var + EPSILON)[:, None]).reshape(FRAMES, ROWS, COLS, CH) * norm_gain + norm_bias
        hidden = jax.nn.silu(normed).astype(jnp.bfloat16)
        hidden_pad = jnp.pad(hidden, ((2, 0), (1, 1), (1, 1), (0, 0)))
        mixed = causal_mix(hidden_pad, conv_weight, conv_bias, FRAMES, ROWS, COLS)
        with_skip = (clip_data.astype(jnp.float32) + mixed).astype(jnp.bfloat16)
        padded = jnp.pad(with_skip, ((0, 0), (0, 1), (0, 1), (0, 0)))
        reduced = strided_mix(padded, down_weight, down_bias, ROWS // 2, COLS // 2).astype(jnp.bfloat16)
        time_pad = jnp.pad(reduced, ((2, 0), (0, 0), (0, 0), (0, 0)))
        lat_mixed = time_mix(time_pad, time_weight, time_bias, LAT_FRAMES).astype(jnp.bfloat16)
        latent = project_head(lat_mixed, head_weight, head_bias)
        return to_tiles(latent)
    patch_tiles = lax.map(encode_clip, inputs)
    flat_rows = (tile_shard * CAP + tile_slot).astype(jnp.int32)
    frame_ids = jnp.arange(LAT_FRAMES, dtype=jnp.int32)[None, :, None] + jnp.zeros_like(flat_rows)
    packed = jnp.zeros((LAT_FRAMES, CLIPS * CAP, 4 * ZCH), jnp.bfloat16)
    return packed.at[frame_ids, flat_rows].set(patch_tiles)
```

```python
import jax
import jax.numpy as jnp
from jax import lax
from jax.sharding import PartitionSpec as P

GROUPS = 32


EPSILON = 1e-06


def causal_mix(stacked_pad, weight, bias_vec, frame_count, row_count, col_count):
    channels = weight.shape[-1]
    col_stack = jnp.concatenate(
        [stacked_pad[:, :, col_tap : col_tap + col_count] for col_tap in range(3)], axis=-1
    )
    accum_sum = jnp.zeros((frame_count * row_count * col_count, channels), jnp.float32)
    for time_tap in range(3):
        for row_tap in range(3):
            stacked = col_stack[time_tap : time_tap + frame_count, row_tap : row_tap + row_count]
            accum_sum = accum_sum + jnp.dot(
                stacked.reshape(-1, 3 * channels),
                weight[time_tap, row_tap].reshape(3 * channels, channels),
                preferred_element_type=jnp.float32,
            )
    return accum_sum.reshape(frame_count, row_count, col_count, channels) + bias_vec


def strided_mix(padded, weight, bias_vec, row_out, col_out):
    frame_count = padded.shape[0]
    channels = weight.shape[-1]
    accum_sum = jnp.zeros((frame_count * row_out * col_out, channels), jnp.float32)
    for row_tap in range(3):
        window = padded[:, row_tap : row_tap + 2 * row_out : 2]
        stacked = jnp.concatenate(
            [window[:, :, col_tap : col_tap + 2 * col_out : 2] for col_tap in range(3)], axis=-1
        )
        accum_sum = accum_sum + jnp.dot(
            stacked.reshape(-1, 3 * channels),
            weight[row_tap].reshape(3 * channels, channels),
            preferred_element_type=jnp.float32,
        )
    return accum_sum.reshape(frame_count, row_out, col_out, channels) + bias_vec


def time_mix(padded, weight, bias_vec, lat_count):
    channels = weight.shape[-1]
    rest = padded.shape[1:3]
    accum_sum = jnp.zeros((lat_count * rest[0] * rest[1], channels), jnp.float32)
    for time_tap in range(3):
        window = padded[time_tap : time_tap + 2 * lat_count - 1 : 2]
        accum_sum = accum_sum + jnp.dot(
            window.reshape(-1, channels), weight[time_tap], preferred_element_type=jnp.float32
        )
    return accum_sum.reshape(lat_count, rest[0], rest[1], channels) + bias_vec


def project_head(lat_mixed, head_weight, head_bias):
    lat_count, row_count, col_count, channels = lat_mixed.shape
    out_channels = head_weight.shape[1]
    latent = (
        jnp.dot(lat_mixed.reshape(-1, channels), head_weight, preferred_element_type=jnp.float32)
        + head_bias
    )
    return latent.astype(jnp.bfloat16).reshape(lat_count, row_count, col_count, out_channels)


def to_tiles(latent):
    lat_count, row_count, col_count, out_channels = latent.shape
    split_up = latent.reshape(lat_count, row_count // 2, 2, col_count // 2, 2, out_channels)
    split_up = split_up.transpose(0, 1, 3, 2, 4, 5)
    return split_up.reshape(lat_count, row_count // 2 * (col_count // 2), 4 * out_channels)


def normalize(block, group_mean, inverse, norm_gain, norm_bias):
    shape_in = block.shape
    grouped = block.astype(jnp.float32).reshape(shape_in[:-1] + (GROUPS, shape_in[-1] // GROUPS))
    normed = ((grouped - group_mean[:, None]) * inverse[:, None]).reshape(shape_in)
    return jax.nn.silu(normed * norm_gain + norm_bias)


def local(
    inputs,
    norm_gain,
    norm_bias,
    conv_weight,
    conv_bias,
    down_weight,
    down_bias,
    time_weight,
    time_bias,
    head_weight,
    head_bias,
    tile_shard,
    tile_slot,
):
    activations = inputs[0]
    frame_count, row_count, col_count, channels = activations.shape
    frame_devs = lax.axis_size("frame")
    position = lax.axis_index("frame")
    per_group = channels // GROUPS
    onward = [(i, i + 1) for i in range(frame_devs - 1)]
    back = [(i + 1, i) for i in range(frame_devs - 1)]
    above = lax.ppermute(activations[:, row_count - 1 :], "frame", onward)
    below = lax.ppermute(activations[:, :2], "frame", back)
    count = frame_count * row_count * col_count
    values = activations.astype(jnp.float32)
    local_sum = jnp.sum(values, axis=(0, 1, 2))
    centred = values - local_sum / count
    local_dev = jnp.sum(centred * centred, axis=(0, 1, 2))
    stats = jnp.broadcast_to(jnp.stack([local_sum, local_dev])[None], (frame_devs, 2, channels))
    stats = lax.all_to_all(stats, "frame", split_axis=0, concat_axis=0, tiled=True)
    sums = stats[:, 0].reshape(frame_devs, GROUPS, per_group)
    devs = stats[:, 1].reshape(frame_devs, GROUPS, per_group)
    entries = count * frame_devs * per_group
    group_mean = jnp.sum(sums, axis=(0, 2)) / entries
    off = sums / count - group_mean[None, :, None]
    group_var = jnp.sum(devs + count * off * off, axis=(0, 2)) / entries
    inverse = lax.rsqrt(group_var + EPSILON)
    rows = jnp.concatenate([above, activations, below], axis=1)
    hidden = normalize(rows, group_mean, inverse, norm_gain, norm_bias)
    row_ids = position * row_count - 1 + jnp.arange(row_count + 3)
    inside = (row_ids >= 0) & (row_ids < frame_devs * row_count)
    hidden = jnp.where(inside[None, :, None, None], hidden, 0.0).astype(jnp.bfloat16)
    hidden_pad = jnp.pad(hidden, ((2, 0), (0, 0), (1, 1), (0, 0)))
    mixed = causal_mix(hidden_pad, conv_weight, conv_bias, frame_count, row_count + 1, col_count)
    with_skip = rows[:, 1 : row_count + 2].astype(jnp.float32) + mixed
    with_skip = jnp.where(inside[None, 1 : row_count + 2, None, None], with_skip, 0.0)
    padded = jnp.pad(with_skip.astype(jnp.bfloat16), ((0, 0), (0, 0), (0, 1), (0, 0)))
    reduced = strided_mix(padded, down_weight, down_bias, row_count // 2, col_count // 2).astype(
        jnp.bfloat16
    )
    time_pad = jnp.pad(reduced, ((2, 0), (0, 0), (0, 0), (0, 0)))
    lat_mixed = time_mix(time_pad, time_weight, time_bias, (frame_count + 1) // 2).astype(
        jnp.bfloat16
    )
    latent = project_head(lat_mixed, head_weight, head_bias)
    patch_tiles = to_tiles(latent)
    lat_count, tile_count, tile_width = patch_tiles.shape
    shards = lax.axis_size("clip")
    slot_block = 2 * shards
    shard_ids = tile_shard[0]
    slot_ids = tile_slot[0] - position * slot_block
    earlier = jnp.arange(tile_count)[None, :, None] > jnp.arange(tile_count)[None, None, :]
    same = shard_ids[:, :, None] == shard_ids[:, None, :]
    rank_in = jnp.sum((same & earlier).astype(jnp.int32), axis=-1)
    pair = 2 * jnp.arange(lat_count, dtype=jnp.int32)[:, None] + rank_in
    target = (shard_ids * 8 + pair).reshape(-1)
    tiles = patch_tiles.reshape(lat_count * tile_count, tile_width)
    chooser = target[None, :] == jnp.arange(8 * shards, dtype=jnp.int32)[:, None]
    outgoing = jnp.dot(
        chooser.astype(jnp.bfloat16), tiles, preferred_element_type=jnp.float32
    ).reshape(shards, 8, tile_width)
    slot_of = jnp.sum(
        jnp.where(chooser, slot_ids.reshape(-1)[None, :] + 1, 0), axis=-1
    ).reshape(shards, 1, 8)
    slot_row = jnp.pad(slot_of, ((0, 0), (0, 0), (0, tile_width - 8))).astype(jnp.float32)
    is_slot = jnp.arange(8)[None, :, None] == 6
    outgoing = jnp.where(is_slot, slot_row, outgoing).astype(jnp.bfloat16)
    arrived = lax.all_to_all(outgoing, "clip", split_axis=0, concat_axis=0, tiled=True)
    slots = arrived[:, 6, :8].astype(jnp.int32)
    want = jnp.arange(lat_count * slot_block, dtype=jnp.int32)
    have = slots - 1 + slot_block * (jnp.arange(8, dtype=jnp.int32) // 2)[None, :]
    have = jnp.where(slots > 0, have, -1).reshape(-1)
    placer = (want[:, None] == have[None, :]).astype(jnp.bfloat16)
    packed = jnp.dot(
        placer, arrived.reshape(8 * shards, tile_width), preferred_element_type=jnp.float32
    )
    return packed.reshape(lat_count, slot_block, tile_width).astype(jnp.bfloat16)


def solution(mesh):
    placed = (
        P("clip", None, "frame", None, None),
        P(),
        P(),
        P(),
        P(),
        P(),
        P(),
        P(),
        P(),
        P(),
        P(),
        P("clip", None, "frame"),
        P("clip", None, "frame"),
    )
    return jax.shard_map(
        local,
        mesh=mesh,
        in_specs=placed,
        out_specs=P(None, ("clip", "frame"), None),
        check_vma=False,
    )
```

```python
import functools

import jax
import jax.numpy as jnp
from jax import lax
from jax.experimental import pallas as pl
from jax.experimental.pallas import tpu as pltpu
from jax.sharding import PartitionSpec as P

GROUPS = 32
EPSILON = 1e-06
PACK = 8
F32 = jnp.float32
BF16 = jnp.bfloat16


def iota(shape, dim):
    return lax.broadcasted_iota(jnp.int32, shape, dim)


def onehot(mask):
    return jnp.where(mask, 1.0, 0.0).astype(BF16)


def matmul(lhs, rhs):
    return jnp.dot(lhs, rhs, preferred_element_type=F32)


def matmul_nt(lhs, rhs):
    return lax.dot_general(lhs, rhs, (((1,), (1,)), ((), ())), preferred_element_type=F32)


def stats_kernel(x_ref, stats_ref, tail_ref, head_ref):
    frames, rows, cols, channels = x_ref.shape
    count = frames * rows * cols
    total = jnp.zeros((8, channels), F32)
    for f in range(frames):
        block = x_ref[f].astype(F32).reshape(-1, 8, channels)
        total = total + jnp.sum(block, axis=0)
    total = jnp.sum(total, axis=0, keepdims=True)
    mean = total / count
    spread = jnp.zeros((8, channels), F32)
    for f in range(frames):
        off = x_ref[f].astype(F32).reshape(-1, 8, channels) - mean
        spread = spread + jnp.sum(off * off, axis=0)
    spread = jnp.sum(spread, axis=0, keepdims=True)
    both = jnp.concatenate([total, spread], axis=0)
    for d in range(stats_ref.shape[0]):
        stats_ref[d] = both
    tail_ref[...] = x_ref[:, rows - 1 :]
    head_ref[...] = x_ref[:, :2]


def over_group(values, width):
    lane = iota(values.shape, 1)
    size = values.shape[1]
    step = 1
    while step < width:
        after = pltpu.roll(values, size - step, 1)
        before = pltpu.roll(values, step, 1)
        values = values + jnp.where((lane // step) % 2 == 0, after, before)
        step *= 2
    return values


def encode_kernel(
    pos_ref, x_ref, up_ref, dn_ref, stats_ref, vec_ref, cw_ref, dw_ref, tw_ref, hw_ref,
    shard_ref, slot_ref, out_ref, raw, hid, skip, red,
):
    frames, rows, cols, channels = x_ref.shape
    pairs = cols // 2
    devices = stats_ref.shape[0]
    per_group = channels // GROUPS
    count = frames * rows * cols
    lats = (frames + 1) // 2
    ext = rows + 3
    made = rows + 1

    stats = stats_ref[...]
    sums, devs = stats[:, 0], stats[:, 1]
    entries = count * devices * per_group
    mean = over_group(jnp.broadcast_to(jnp.sum(sums, axis=0, keepdims=True), (8, channels)), per_group)
    mean = mean[:1] / entries
    off = sums / count - mean
    var = jnp.sum(devs + count * (off * off), axis=0, keepdims=True)
    var = over_group(jnp.broadcast_to(var, (8, channels)), per_group)[:1] / entries
    scale = lax.rsqrt(var + EPSILON) * vec_ref[0:1] * 0.5
    shift = vec_ref[1:2] * 0.5

    place = pos_ref[0]
    has_up = jnp.where(place > 0, 1.0, 0.0).astype(F32)
    has_dn = jnp.where(place < devices - 1, 1.0, 0.0).astype(F32)

    def row(f, r):
        if r == 0:
            return up_ref[f, 0]
        if r <= rows:
            return x_ref[f, r - 1]
        return dn_ref[f, r - 1 - rows]

    pair_id = iota((pairs, channels), 0)
    conv_bias = vec_ref[2:3]
    for f in range(frames):
        for r in range(ext):
            raw[f, r] = row(f, r).astype(F32)
            halves = []
            for parity in range(2):
                half = (raw[f, r, pl.ds(parity, pairs, stride=2), :] - mean) * scale + shift
                half = half + half * jnp.tanh(half)
                if r == 0:
                    half = half * has_up
                elif r > rows:
                    half = half * has_dn
                halves.append(half)
            even, odd = halves
            left = jnp.where(pair_id == 0, 0.0, pltpu.roll(odd, 1, 0))
            right = jnp.where(pair_id == pairs - 1, 0.0, pltpu.roll(even, pairs - 1, 0))
            for u, part in enumerate((left, even, odd, right)):
                hid[f, r, :, u * channels : (u + 1) * channels] = part.astype(BF16)

    none = jnp.zeros((channels, channels), BF16)

    def pair_weight(a, b):
        w = [cw_ref[a, b, e] for e in range(3)]
        return jnp.concatenate(
            [
                jnp.concatenate([w[0], w[1], w[2], none], axis=0),
                jnp.concatenate([none, w[0], w[1], w[2]], axis=0),
            ],
            axis=1,
        )

    for f in range(frames):
        acc = jnp.zeros((made * pairs, 2 * channels), F32)
        for a in range(3):
            g = f - 2 + a
            if g < 0:
                continue
            for b in range(3):
                lhs = hid[g, b : b + made].reshape(made * pairs, 4 * channels)
                acc = acc + matmul(lhs, pair_weight(a, b))
        for r in range(made):
            block = acc[r * pairs : (r + 1) * pairs]
            ends = []
            for parity in range(2):
                half = block[:, parity * channels : (parity + 1) * channels] + conv_bias
                half = half + raw[f, r + 1, pl.ds(parity, pairs, stride=2), :]
                if r == rows:
                    half = half * has_dn
                ends.append(half)
            right = jnp.where(pair_id == pairs - 1, 0.0, pltpu.roll(ends[0], pairs - 1, 0))
            for u, part in enumerate((*ends, right)):
                skip[f, r, :, u * channels : (u + 1) * channels] = part.astype(BF16)

    down = jnp.concatenate([dw_ref[b, e] for b in range(3) for e in range(3)], axis=0)
    spots = rows // 2 * pairs
    for f in range(frames):
        lhs = jnp.concatenate(
            [
                jnp.concatenate([skip[f, 2 * i + b] for i in range(rows // 2)], axis=0)
                for b in range(3)
            ],
            axis=1,
        )
        red[f] = (matmul(lhs, down) + vec_ref[3:4]).astype(BF16)

    blank = jnp.zeros((spots, channels), BF16)
    taps = jnp.concatenate(
        [
            jnp.concatenate(
                [red[2 * l - 2 + k] if 2 * l - 2 + k >= 0 else blank for k in range(3)], axis=1
            )
            for l in range(lats)
        ],
        axis=0,
    )
    mixing = jnp.concatenate([tw_ref[k] for k in range(3)], axis=0)
    mixed = (matmul(taps, mixing) + vec_ref[4:5]).astype(BF16)
    width = hw_ref.shape[1]
    copies = channels // width
    spread = onehot(iota((width, channels), 1) % width == iota((width, channels), 0))
    head = matmul(hw_ref[...], spread).astype(BF16)
    latent = matmul(mixed, head) + vec_ref[5:6]
    spot = iota(latent.shape, 0) % spots
    corner = (spot // pairs) % 2 * 2 + spot % 2
    latent = jnp.where(iota(latent.shape, 1) // width == corner, latent, 0.0).astype(BF16)

    tiles = shard_ref.shape[2]
    shards = out_ref.shape[0] // PACK
    slot_base = place * (2 * shards)
    upper = onehot(iota((tiles, tiles), 0) < iota((tiles, tiles), 1))
    half_pairs = pairs // 2
    at = iota((tiles, spots), 1)
    grown = onehot(at // (2 * pairs) * half_pairs + at % pairs // 2 == iota((tiles, spots), 0))
    out = jnp.zeros(out_ref.shape, F32)
    slots = jnp.zeros((shards, channels), F32)
    for l in range(lats):
        shard = jnp.broadcast_to(shard_ref[0, l : l + 1], (shards, tiles))
        mine = shard == iota((shards, tiles), 0)
        earlier = matmul(onehot(mine), upper)
        rank = jnp.sum(jnp.where(mine, earlier, 0.0), axis=0, keepdims=True)
        key = shard_ref[0, l : l + 1].astype(F32) * PACK + 2 * l + rank
        key = matmul(jnp.broadcast_to(key, (8, tiles)).astype(BF16), grown)[:1].astype(jnp.int32)
        chosen = onehot(iota((out_ref.shape[0], spots), 0) == key)
        out = out + matmul(chosen, latent[l * spots : (l + 1) * spots])
        number = jnp.broadcast_to(slot_ref[0, l : l + 1] - slot_base + 1, (shards, tiles))
        number = jnp.where(mine, number.astype(F32), 0.0).astype(BF16)
        which = jnp.broadcast_to(rank.astype(jnp.int32) + 2 * l, (channels, tiles))
        slots = slots + matmul_nt(number, onehot(which == iota((channels, tiles), 0)))
    line = iota((out_ref.shape[0], shards), 0)
    put = onehot((line % PACK == PACK - 2) & (line // PACK == iota(line.shape, 1)))
    out_ref[...] = (out + matmul(put, slots.astype(BF16))).astype(BF16)


def place_kernel(got_ref, out_ref):
    lines, width = got_ref.shape
    slots = out_ref.shape[0]
    got = got_ref[...]
    here, there = iota((lines, lines), 0), iota((lines, lines), 1)
    table = matmul(onehot(there == here // PACK * PACK + PACK - 2), got)
    own = iota(table.shape, 0) % PACK
    table = jnp.where((iota(table.shape, 1) == own) & (own < PACK - 2), table, 0.0).astype(BF16)
    slot = matmul_nt(jnp.ones((8, width), BF16), table)[:1].astype(jnp.int32)
    line = iota((1, lines), 1)
    per_lat = slots // ((PACK - 2) // 2)
    want = jnp.where(slot > 0, slot - 1 + line % PACK // 2 * per_lat, -1)
    out_ref[...] = matmul(onehot(iota((slots, lines), 0) == want), got).astype(BF16)


def vmem(count):
    return [pl.BlockSpec(memory_space=pltpu.VMEM)] * count


def local(
    inputs,
    norm_gain,
    norm_bias,
    conv_weight,
    conv_bias,
    down_weight,
    down_bias,
    time_weight,
    time_bias,
    head_weight,
    head_bias,
    tile_shard,
    tile_slot,
):
    activations = inputs[0]
    frames, rows, cols, channels = activations.shape
    devices = lax.axis_size("frame")
    shards = lax.axis_size("clip")
    lats = (frames + 1) // 2
    position = lax.axis_index("frame").astype(jnp.int32).reshape(1)

    stats, tail, head = pl.pallas_call(
        stats_kernel,
        out_shape=(
            jax.ShapeDtypeStruct((devices, 2, channels), F32),
            jax.ShapeDtypeStruct((frames, 1, cols, channels), BF16),
            jax.ShapeDtypeStruct((frames, 2, cols, channels), BF16),
        ),
        in_specs=vmem(1),
        out_specs=tuple(vmem(3)),
        compiler_params=pltpu.CompilerParams(vmem_limit_bytes=8 << 20),
        name="stats",
    )(activations)
    stats = lax.all_to_all(stats, "frame", split_axis=0, concat_axis=0, tiled=True)
    above = lax.ppermute(tail, "frame", [(i, i + 1) for i in range(devices - 1)])
    below = lax.ppermute(head, "frame", [(i + 1, i) for i in range(devices - 1)])
    vectors = jnp.stack(
        [
            norm_gain,
            norm_bias,
            conv_bias,
            down_bias,
            time_bias,
            jnp.tile(head_bias, channels // head_bias.shape[0]),
            norm_gain,
            norm_gain,
        ]
    )
    outgoing = pl.pallas_call(
        encode_kernel,
        out_shape=jax.ShapeDtypeStruct((shards * PACK, channels), BF16),
        in_specs=[pl.BlockSpec(memory_space=pltpu.SMEM), *vmem(11)],
        out_specs=pl.BlockSpec(memory_space=pltpu.VMEM),
        scratch_shapes=[
            pltpu.VMEM((frames, rows + 3, cols, channels), F32),
            pltpu.VMEM((frames, rows + 3, cols // 2, 4 * channels), BF16),
            pltpu.VMEM((frames, rows + 1, cols // 2, 3 * channels), BF16),
            pltpu.VMEM((frames, rows // 2 * (cols // 2), channels), BF16),
        ],
        compiler_params=pltpu.CompilerParams(vmem_limit_bytes=32 << 20),
        name="encode",
    )(
        position, activations, above, below, stats, vectors, conv_weight, down_weight,
        time_weight, head_weight, tile_shard, tile_slot,
    )
    arrived = lax.all_to_all(
        outgoing.reshape(shards, PACK, channels), "clip", split_axis=0, concat_axis=0, tiled=True
    )
    packed = pl.pallas_call(
        place_kernel,
        out_shape=jax.ShapeDtypeStruct((lats * 2 * shards, channels), BF16),
        in_specs=vmem(1),
        out_specs=pl.BlockSpec(memory_space=pltpu.VMEM),
        compiler_params=pltpu.CompilerParams(vmem_limit_bytes=8 << 20),
        name="place",
    )(arrived.reshape(shards * PACK, channels))
    return packed.reshape(lats, 2 * shards, channels)


def solution(mesh):
    placed = (
        P("clip", None, "frame", None, None),
        P(),
        P(),
        P(),
        P(),
        P(),
        P(),
        P(),
        P(),
        P(),
        P(),
        P("clip", None, "frame"),
        P("clip", None, "frame"),
    )
    return jax.shard_map(
        local,
        mesh=mesh,
        in_specs=placed,
        out_specs=P(None, ("clip", "frame"), None),
        check_vma=False,
    )
```

```python
import functools

import jax
import jax.numpy as jnp
from jax import lax
from jax.experimental import pallas as pl
from jax.experimental.pallas import tpu as pltpu
from jax.sharding import PartitionSpec as P

GROUPS = 32
EPSILON = 1e-06
PACK = 8
F32 = jnp.float32
BF16 = jnp.bfloat16


def iota(shape, dim):
    return lax.broadcasted_iota(jnp.int32, shape, dim)


def onehot(mask):
    return jnp.where(mask, 1.0, 0.0).astype(BF16)


def matmul(lhs, rhs):
    return jnp.dot(lhs, rhs, preferred_element_type=F32)


def matmul_nt(lhs, rhs):
    return lax.dot_general(lhs, rhs, (((1,), (1,)), ((), ())), preferred_element_type=F32)


def stats_kernel(x_ref, stats_ref, tail_ref, head_ref):
    frames, rows, cols, channels = x_ref.shape
    count = frames * rows * cols

    def over_all(change):
        parts = [jnp.sum(change(x_ref[f].astype(F32)), axis=0) for f in range(frames)]
        return jnp.sum(sum(parts), axis=0, keepdims=True)

    total = over_all(lambda v: v)
    mean = total / count
    spread = over_all(lambda v: (v - mean) * (v - mean))
    both = jnp.concatenate([total, spread], axis=0)
    for d in range(stats_ref.shape[0]):
        stats_ref[d] = both
    tail_ref[...] = x_ref[:, rows - 1 :]
    head_ref[...] = x_ref[:, :2]


def over_group(values, width):
    lane = iota(values.shape, 1)
    size = values.shape[1]
    step = 1
    while step < width:
        after = pltpu.roll(values, size - step, 1)
        before = pltpu.roll(values, step, 1)
        values = values + jnp.where((lane // step) % 2 == 0, after, before)
        step *= 2
    return values


def encode_kernel(
    pos_ref, x_ref, up_ref, dn_ref, stats_ref, vec_ref, head_ref, keys_ref, slots_ref, cw_ref,
    dw_ref, tw_ref, out_ref, raw, hid, skip, red,
):
    frames, rows, cols, channels = x_ref.shape
    pairs = cols // 2
    devices = stats_ref.shape[0]
    per_group = channels // GROUPS
    count = frames * rows * cols
    lats = (frames + 1) // 2
    ext = rows + 3
    made = rows + 1

    stats = stats_ref[...]
    sums, devs = stats[:, 0], stats[:, 1]
    entries = count * devices * per_group
    mean = over_group(jnp.broadcast_to(jnp.sum(sums, axis=0, keepdims=True), (8, channels)), per_group)
    mean = mean[:1] / entries
    off = sums / count - mean
    var = jnp.sum(devs + count * (off * off), axis=0, keepdims=True)
    var = over_group(jnp.broadcast_to(var, (8, channels)), per_group)[:1] / entries
    scale = lax.rsqrt(var + EPSILON) * vec_ref[0:1] * 0.5
    shift = vec_ref[1:2] * 0.5

    place = pos_ref[0]
    has_up = jnp.where(place > 0, 1.0, 0.0).astype(F32)
    has_dn = jnp.where(place < devices - 1, 1.0, 0.0).astype(F32)

    def row(f, r):
        if r == 0:
            return up_ref[f, 0]
        if r <= rows:
            return x_ref[f, r - 1]
        return dn_ref[f, r - 1 - rows]

    pair_id = iota((pairs, channels), 0)
    conv_bias = vec_ref[2:3]
    for f in range(frames):
        for r in range(ext):
            raw[f, r] = row(f, r).astype(F32)
            halves = []
            for parity in range(2):
                half = (raw[f, r, pl.ds(parity, pairs, stride=2), :] - mean) * scale + shift
                half = half + half * jnp.tanh(half)
                if r == 0:
                    half = half * has_up
                elif r > rows:
                    half = half * has_dn
                halves.append(half)
            even, odd = halves
            left = jnp.where(pair_id == 0, 0.0, pltpu.roll(odd, 1, 0))
            right = jnp.where(pair_id == pairs - 1, 0.0, pltpu.roll(even, pairs - 1, 0))
            for u, part in enumerate((left, even, odd, right)):
                hid[f, r, :, u * channels : (u + 1) * channels] = part.astype(BF16)

    none = jnp.zeros((channels, channels), BF16)

    def pair_weight(a, b):
        w = [cw_ref[a, b, e] for e in range(3)]
        return jnp.concatenate(
            [
                jnp.concatenate([w[0], w[1], w[2], none], axis=0),
                jnp.concatenate([none, w[0], w[1], w[2]], axis=0),
            ],
            axis=1,
        )

    for f in range(frames):
        acc = jnp.zeros((made * pairs, 2 * channels), F32)
        for a in range(3):
            g = f - 2 + a
            if g < 0:
                continue
            for b in range(3):
                lhs = hid[g, b : b + made].reshape(made * pairs, 4 * channels)
                acc = acc + matmul(lhs, pair_weight(a, b))
        for r in range(made):
            block = acc[r * pairs : (r + 1) * pairs]
            ends = []
            for parity in range(2):
                half = block[:, parity * channels : (parity + 1) * channels] + conv_bias
                half = half + raw[f, r + 1, pl.ds(parity, pairs, stride=2), :]
                if r == rows:
                    half = half * has_dn
                ends.append(half)
            right = jnp.where(pair_id == pairs - 1, 0.0, pltpu.roll(ends[0], pairs - 1, 0))
            for u, part in enumerate((*ends, right)):
                skip[f, r, :, u * channels : (u + 1) * channels] = part.astype(BF16)

    down = jnp.concatenate([dw_ref[b, e] for b in range(3) for e in range(3)], axis=0)
    spots = rows // 2 * pairs
    for f in range(frames):
        lhs = jnp.concatenate(
            [
                jnp.concatenate([skip[f, 2 * i + b] for i in range(rows // 2)], axis=0)
                for b in range(3)
            ],
            axis=1,
        )
        red[f] = (matmul(lhs, down) + vec_ref[3:4]).astype(BF16)

    blank = jnp.zeros((spots, channels), BF16)
    taps = jnp.concatenate(
        [
            jnp.concatenate(
                [red[2 * l - 2 + k] if 2 * l - 2 + k >= 0 else blank for k in range(3)], axis=1
            )
            for l in range(lats)
        ],
        axis=0,
    )
    mixing = jnp.concatenate([tw_ref[k] for k in range(3)], axis=0)
    mixed = (matmul(taps, mixing) + vec_ref[4:5]).astype(BF16)
    width = channels // 4
    latent = matmul_nt(mixed, head_ref[...]) + vec_ref[5:6]
    spot = iota(latent.shape, 0) % spots
    corner = (spot // pairs) % 2 * 2 + spot % 2
    latent = jnp.where(iota(latent.shape, 1) // width == corner, latent, 0.0).astype(BF16)

    line = iota((out_ref.shape[0], spots), 0)
    out = put_slots(slots_ref[...], out_ref.shape[0])
    for l in range(lats):
        chosen = onehot(line == keys_ref[l : l + 1])
        out = out + matmul(chosen, latent[l * spots : (l + 1) * spots])
    out_ref[...] = out.astype(BF16)


def put_slots(slots, lines):
    line = iota((lines, slots.shape[0]), 0)
    put = onehot((line % PACK == PACK - 2) & (line // PACK == iota(line.shape, 1)))
    return matmul(put, slots)


def prep_kernel(*refs, pairs):
    pos_ref, shard_ref, slot_ref, *line_refs, hw_ref = refs[:-4]
    keys_ref, slots_ref, vec_ref, head_ref = refs[-4:]
    copies = vec_ref.shape[1] // hw_ref.shape[0]
    for i, ref in enumerate(line_refs):
        row = ref[...]
        if row.shape[1] < vec_ref.shape[1]:
            row = jnp.concatenate([row] * copies, axis=1)
        vec_ref[i : i + 1] = row
    vec_ref[len(line_refs) :] = jnp.zeros((8 - len(line_refs), vec_ref.shape[1]), F32)
    head_ref[...] = jnp.concatenate([hw_ref[...]] * copies, axis=0)
    lats, _, tiles = shard_ref.shape
    shards, channels = slots_ref.shape
    spots = keys_ref.shape[1]
    slot_base = pos_ref[0] * (2 * shards)
    upper = onehot(iota((tiles, tiles), 0) < iota((tiles, tiles), 1))
    at = iota((tiles, spots), 1)
    grown = at // (2 * pairs) * (pairs // 2) + at % pairs // 2
    grown = onehot(grown == iota((tiles, spots), 0))
    slots = jnp.zeros((shards, channels), F32)
    keys = []
    for l in range(lats):
        shard = jnp.broadcast_to(shard_ref[l], (shards, tiles))
        mine = shard == iota((shards, tiles), 0)
        earlier = matmul(onehot(mine), upper)
        rank = jnp.sum(jnp.where(mine, earlier, 0.0), axis=0, keepdims=True)
        keys.append(shard_ref[l].astype(F32) * PACK + 2 * l + rank)
        number = jnp.broadcast_to(slot_ref[l] - slot_base + 1, (shards, tiles))
        number = jnp.where(mine, number.astype(F32), 0.0).astype(BF16)
        which = jnp.broadcast_to(rank.astype(jnp.int32) + 2 * l, (channels, tiles))
        slots = slots + matmul_nt(number, onehot(which == iota((channels, tiles), 0) % PACK))
    keys = jnp.concatenate(keys + [jnp.zeros((8 - lats, tiles), F32)], axis=0)
    keys_ref[...] = matmul(keys.astype(BF16), grown).astype(jnp.int32)
    slots_ref[...] = slots.astype(BF16)


def place_kernel(got_ref, out_ref):
    lines, width = got_ref.shape
    slots = out_ref.shape[0]
    shards = lines // PACK
    got = got_ref[...]
    pick = iota((shards, lines), 1) == iota((shards, lines), 0) * PACK + PACK - 2
    table = matmul(onehot(pick), got)
    table = jnp.concatenate([table] * (lines // width), axis=1)
    table = jnp.where(iota(table.shape, 1) // PACK == iota(table.shape, 0), table, 0.0)
    slot = jnp.sum(table, axis=0, keepdims=True).astype(jnp.int32)
    own = iota((1, lines), 1) % PACK
    per_lat = slots // ((PACK - 2) // 2)
    want = jnp.where((slot > 0) & (own < PACK - 2), slot - 1 + own // 2 * per_lat, -1)
    out_ref[...] = matmul(onehot(iota((slots, lines), 0) == want), got).astype(BF16)


def vmem(count):
    return [pl.BlockSpec(memory_space=pltpu.VMEM)] * count


def local(
    inputs,
    norm_gain,
    norm_bias,
    conv_weight,
    conv_bias,
    down_weight,
    down_bias,
    time_weight,
    time_bias,
    head_weight,
    head_bias,
    tile_shard,
    tile_slot,
):
    activations = inputs[0]
    frames, rows, cols, channels = activations.shape
    devices = lax.axis_size("frame")
    shards = lax.axis_size("clip")
    lats = (frames + 1) // 2
    position = lax.axis_index("frame").astype(jnp.int32).reshape(1)

    stats, tail, head = pl.pallas_call(
        stats_kernel,
        out_shape=(
            jax.ShapeDtypeStruct((devices, 2, channels), F32),
            jax.ShapeDtypeStruct((frames, 1, cols, channels), BF16),
            jax.ShapeDtypeStruct((frames, 2, cols, channels), BF16),
        ),
        in_specs=vmem(1),
        out_specs=tuple(vmem(3)),
        compiler_params=pltpu.CompilerParams(vmem_limit_bytes=8 << 20),
        name="stats",
    )(activations)
    stats = lax.all_to_all(stats, "frame", split_axis=0, concat_axis=0, tiled=True)
    above = lax.ppermute(tail, "frame", [(i, i + 1) for i in range(devices - 1)])
    below = lax.ppermute(head, "frame", [(i + 1, i) for i in range(devices - 1)])
    lines = [
        v.reshape(1, -1)
        for v in (norm_gain, norm_bias, conv_bias, down_bias, time_bias, head_bias)
    ]
    pairs = cols // 2
    prepared = pl.pallas_call(
        functools.partial(prep_kernel, pairs=pairs),
        out_shape=(
            jax.ShapeDtypeStruct((8, rows // 2 * pairs), jnp.int32),
            jax.ShapeDtypeStruct((shards, channels), BF16),
            jax.ShapeDtypeStruct((8, channels), F32),
            jax.ShapeDtypeStruct((channels, channels), BF16),
        ),
        in_specs=[pl.BlockSpec(memory_space=pltpu.SMEM), *vmem(9)],
        out_specs=tuple(vmem(4)),
        compiler_params=pltpu.CompilerParams(vmem_limit_bytes=4 << 20),
        cost_estimate=pl.CostEstimate(flops=20_000_000_000, bytes_accessed=0, transcendentals=0),
        name="prep",
    )(position, tile_shard.transpose(1, 0, 2), tile_slot.transpose(1, 0, 2), *lines, head_weight.T)
    weights = (conv_weight, down_weight, time_weight)
    outgoing = pl.pallas_call(
        encode_kernel,
        out_shape=jax.ShapeDtypeStruct((shards * PACK, channels), BF16),
        in_specs=[
            pl.BlockSpec(memory_space=pltpu.SMEM),
            *vmem(11),
        ],
        out_specs=pl.BlockSpec(memory_space=pltpu.VMEM),
        scratch_shapes=[
            pltpu.VMEM((frames, rows + 3, cols, channels), F32),
            pltpu.VMEM((frames, rows + 3, cols // 2, 4 * channels), BF16),
            pltpu.VMEM((frames, rows + 1, cols // 2, 3 * channels), BF16),
            pltpu.VMEM((frames, rows // 2 * (cols // 2), channels), BF16),
        ],
        compiler_params=pltpu.CompilerParams(vmem_limit_bytes=32 << 20),
        name="encode",
    )(
        position, activations, above, below, stats, prepared[2], prepared[3], *prepared[:2], *weights
    )
    arrived = lax.all_to_all(
        outgoing.reshape(shards, PACK, channels), "clip", split_axis=0, concat_axis=0, tiled=True
    )
    packed = pl.pallas_call(
        place_kernel,
        out_shape=jax.ShapeDtypeStruct((lats * 2 * shards, channels), BF16),
        in_specs=vmem(1),
        out_specs=pl.BlockSpec(memory_space=pltpu.VMEM),
        compiler_params=pltpu.CompilerParams(vmem_limit_bytes=8 << 20),
        name="place",
    )(arrived.reshape(shards * PACK, channels))
    return packed.reshape(lats, 2 * shards, channels)


def solution(mesh):
    placed = (
        P("clip", None, "frame", None, None),
        P(),
        P(),
        P(),
        P(),
        P(),
        P(),
        P(),
        P(),
        P(),
        P(),
        P("clip", None, "frame"),
        P("clip", None, "frame"),
    )
    return jax.shard_map(
        local,
        mesh=mesh,
        in_specs=placed,
        out_specs=P(None, ("clip", "frame"), None),
        check_vma=False,
    )
```

```python
import functools

import jax
import jax.numpy as jnp
from jax import lax
from jax.experimental import pallas as pl
from jax.experimental.pallas import tpu as pltpu
from jax.sharding import PartitionSpec as P

GROUPS = 32
EPSILON = 1e-06
PACK = 8
F32 = jnp.float32
BF16 = jnp.bfloat16


def iota(shape, dim):
    return lax.broadcasted_iota(jnp.int32, shape, dim)


def onehot(mask):
    return jnp.where(mask, 1.0, 0.0).astype(BF16)


def matmul(lhs, rhs):
    return jnp.dot(lhs, rhs, preferred_element_type=F32)


def matmul_nt(lhs, rhs):
    return lax.dot_general(lhs, rhs, (((1,), (1,)), ((), ())), preferred_element_type=F32)


def stats_kernel(x_ref, stats_ref, tail_ref, head_ref):
    frames, rows, cols, channels = x_ref.shape
    count = frames * rows * cols

    def over_all(change):
        parts = [jnp.sum(change(x_ref[f].astype(F32)), axis=0) for f in range(frames)]
        return jnp.sum(sum(parts), axis=0, keepdims=True)

    total = over_all(lambda v: v)
    mean = total / count
    spread = over_all(lambda v: (v - mean) * (v - mean))
    both = jnp.concatenate([total, spread], axis=0)
    for d in range(stats_ref.shape[0]):
        stats_ref[d] = both
    tail_ref[...] = x_ref[:, rows - 1 :]
    head_ref[...] = x_ref[:, :2]


def over_group(values, width):
    lane = iota(values.shape, 1)
    size = values.shape[1]
    step = 1
    while step < width:
        after = pltpu.roll(values, size - step, 1)
        before = pltpu.roll(values, step, 1)
        values = values + jnp.where((lane // step) % 2 == 0, after, before)
        step *= 2
    return values


def encode_kernel(
    pos_ref, x_ref, up_ref, dn_ref, stats_ref, vec_ref, mix_ref, keys_ref, slots_ref, cw_ref,
    dw_ref, out_ref, raw, hid, skip, red,
):
    frames, rows, cols, channels = x_ref.shape
    pairs = cols // 2
    devices = stats_ref.shape[0]
    per_group = channels // GROUPS
    count = frames * rows * cols
    lats = (frames + 1) // 2
    ext = rows + 3
    made = rows + 1

    stats = stats_ref[...]
    sums, devs = stats[:, 0], stats[:, 1]
    entries = count * devices * per_group
    mean = over_group(jnp.broadcast_to(jnp.sum(sums, axis=0, keepdims=True), (8, channels)), per_group)
    mean = mean[:1] / entries
    off = sums / count - mean
    var = jnp.sum(devs + count * (off * off), axis=0, keepdims=True)
    var = over_group(jnp.broadcast_to(var, (8, channels)), per_group)[:1] / entries
    scale = lax.rsqrt(var + EPSILON) * vec_ref[0:1] * 0.5
    shift = vec_ref[1:2] * 0.5

    place = pos_ref[0]
    has_up = jnp.where(place > 0, 1.0, 0.0).astype(F32)
    has_dn = jnp.where(place < devices - 1, 1.0, 0.0).astype(F32)

    def row(f, r):
        if r == 0:
            return up_ref[f, 0]
        if r <= rows:
            return x_ref[f, r - 1]
        return dn_ref[f, r - 1 - rows]

    pair_id = iota((pairs, channels), 0)
    conv_bias = vec_ref[2:3]
    for f in range(frames):
        for r in range(ext):
            raw[f, r] = row(f, r).astype(F32)
            halves = []
            for parity in range(2):
                half = (raw[f, r, pl.ds(parity, pairs, stride=2), :] - mean) * scale + shift
                half = half + half * jnp.tanh(half)
                if r == 0:
                    half = half * has_up
                elif r > rows:
                    half = half * has_dn
                halves.append(half)
            even, odd = halves
            left = jnp.where(pair_id == 0, 0.0, pltpu.roll(odd, 1, 0))
            right = jnp.where(pair_id == pairs - 1, 0.0, pltpu.roll(even, pairs - 1, 0))
            for u, part in enumerate((left, even, odd, right)):
                hid[f, r, :, u * channels : (u + 1) * channels] = part.astype(BF16)

    none = jnp.zeros((channels, channels), BF16)

    def pair_weight(a, b):
        w = [cw_ref[a, b, e] for e in range(3)]
        return jnp.concatenate(
            [
                jnp.concatenate([w[0], w[1], w[2], none], axis=0),
                jnp.concatenate([none, w[0], w[1], w[2]], axis=0),
            ],
            axis=1,
        )

    for f in range(frames):
        acc = jnp.zeros((made * pairs, 2 * channels), F32)
        for a in range(3):
            g = f - 2 + a
            if g < 0:
                continue
            for b in range(3):
                lhs = hid[g, b : b + made].reshape(made * pairs, 4 * channels)
                acc = acc + matmul(lhs, pair_weight(a, b))
        for r in range(made):
            block = acc[r * pairs : (r + 1) * pairs]
            ends = []
            for parity in range(2):
                half = block[:, parity * channels : (parity + 1) * channels] + conv_bias
                half = half + raw[f, r + 1, pl.ds(parity, pairs, stride=2), :]
                if r == rows:
                    half = half * has_dn
                ends.append(half)
            right = jnp.where(pair_id == pairs - 1, 0.0, pltpu.roll(ends[0], pairs - 1, 0))
            for u, part in enumerate((*ends, right)):
                skip[f, r, :, u * channels : (u + 1) * channels] = part.astype(BF16)

    down = jnp.concatenate([dw_ref[b, e] for b in range(3) for e in range(3)], axis=0)
    spots = rows // 2 * pairs
    for f in range(frames):
        lhs = jnp.concatenate(
            [
                jnp.concatenate([skip[f, 2 * i + b] for i in range(rows // 2)], axis=0)
                for b in range(3)
            ],
            axis=1,
        )
        red[f] = (matmul(lhs, down) + vec_ref[3:4]).astype(BF16)

    blank = jnp.zeros((spots, channels), BF16)
    taps = jnp.concatenate(
        [
            jnp.concatenate(
                [red[2 * l - 2 + k] if 2 * l - 2 + k >= 0 else blank for k in range(3)], axis=1
            )
            for l in range(lats)
        ],
        axis=0,
    )
    width = channels // 4
    latent = matmul(taps, mix_ref[...]) + vec_ref[4:5]
    spot = iota(latent.shape, 0) % spots
    corner = (spot // pairs) % 2 * 2 + spot % 2
    latent = jnp.where(iota(latent.shape, 1) // width == corner, latent, 0.0).astype(BF16)

    line = iota((out_ref.shape[0], spots), 0)
    chosen = [onehot(line == keys_ref[l : l + 1]) for l in range(lats)]
    out = matmul(jnp.concatenate(chosen, axis=1), latent)
    out_ref[...] = (out + put_slots(slots_ref[...], out_ref.shape[0])).astype(BF16)


def put_slots(slots, lines):
    line = iota((lines, slots.shape[0]), 0)
    put = onehot((line % PACK == PACK - 2) & (line // PACK == iota(line.shape, 1)))
    return matmul(put, slots)


def prep_kernel(*refs, pairs):
    pos_ref, shard_ref, slot_ref, *line_refs, hw_ref, tw_ref = refs[:-4]
    keys_ref, slots_ref, vec_ref, mix_ref = refs[-4:]
    for i, ref in enumerate(line_refs[:4]):
        vec_ref[i : i + 1] = ref[...]
    channels = vec_ref.shape[1]
    copies = channels // hw_ref.shape[0]
    head = jnp.concatenate([hw_ref[...]] * copies, axis=0)
    for k in range(3):
        mix_ref[k * channels : (k + 1) * channels] = matmul_nt(tw_ref[k], head).astype(BF16)
    time_bias = lax.dot_general(
        jnp.broadcast_to(line_refs[4][...], (8, channels)),
        head.astype(F32),
        (((1,), (1,)), ((), ())),
        precision=lax.Precision.HIGHEST,
        preferred_element_type=F32,
    )
    head_bias = jnp.concatenate([line_refs[5][...]] * copies, axis=1)
    vec_ref[4:] = jnp.broadcast_to(time_bias[:1] + head_bias, (4, channels))
    lats, _, tiles = shard_ref.shape
    shards, channels = slots_ref.shape
    spots = keys_ref.shape[1]
    slot_base = pos_ref[0] * (2 * shards)
    upper = onehot(iota((tiles, tiles), 0) < iota((tiles, tiles), 1))
    at = iota((tiles, spots), 1)
    grown = at // (2 * pairs) * (pairs // 2) + at % pairs // 2
    grown = onehot(grown == iota((tiles, spots), 0))
    slots = jnp.zeros((shards, channels), F32)
    keys = []
    for l in range(lats):
        shard = jnp.broadcast_to(shard_ref[l], (shards, tiles))
        mine = shard == iota((shards, tiles), 0)
        earlier = matmul(onehot(mine), upper)
        rank = jnp.sum(jnp.where(mine, earlier, 0.0), axis=0, keepdims=True)
        keys.append(shard_ref[l].astype(F32) * PACK + 2 * l + rank)
        number = jnp.broadcast_to(slot_ref[l] - slot_base + 1, (shards, tiles))
        number = jnp.where(mine, number.astype(F32), 0.0).astype(BF16)
        which = jnp.broadcast_to(rank.astype(jnp.int32) + 2 * l, (channels, tiles))
        slots = slots + matmul_nt(number, onehot(which == iota((channels, tiles), 0) % PACK))
    keys = jnp.concatenate(keys + [jnp.zeros((8 - lats, tiles), F32)], axis=0)
    keys_ref[...] = matmul(keys.astype(BF16), grown).astype(jnp.int32)
    slots_ref[...] = slots.astype(BF16)


def place_kernel(got_ref, out_ref):
    lines, width = got_ref.shape
    slots = out_ref.shape[0]
    shards = lines // PACK
    got = got_ref[...]
    pick = iota((shards, lines), 1) == iota((shards, lines), 0) * PACK + PACK - 2
    table = matmul(onehot(pick), got)
    table = jnp.concatenate([table] * (lines // width), axis=1)
    table = jnp.where(iota(table.shape, 1) // PACK == iota(table.shape, 0), table, 0.0)
    slot = jnp.sum(table, axis=0, keepdims=True).astype(jnp.int32)
    own = iota((1, lines), 1) % PACK
    per_lat = slots // ((PACK - 2) // 2)
    want = jnp.where((slot > 0) & (own < PACK - 2), slot - 1 + own // 2 * per_lat, -1)
    out_ref[...] = matmul(onehot(iota((slots, lines), 0) == want), got).astype(BF16)


def vmem(count):
    return [pl.BlockSpec(memory_space=pltpu.VMEM)] * count


def local(
    inputs,
    norm_gain,
    norm_bias,
    conv_weight,
    conv_bias,
    down_weight,
    down_bias,
    time_weight,
    time_bias,
    head_weight,
    head_bias,
    tile_shard,
    tile_slot,
):
    activations = inputs[0]
    frames, rows, cols, channels = activations.shape
    devices = lax.axis_size("frame")
    shards = lax.axis_size("clip")
    lats = (frames + 1) // 2
    position = lax.axis_index("frame").astype(jnp.int32).reshape(1)

    stats, tail, head = pl.pallas_call(
        stats_kernel,
        out_shape=(
            jax.ShapeDtypeStruct((devices, 2, channels), F32),
            jax.ShapeDtypeStruct((frames, 1, cols, channels), BF16),
            jax.ShapeDtypeStruct((frames, 2, cols, channels), BF16),
        ),
        in_specs=vmem(1),
        out_specs=tuple(vmem(3)),
        compiler_params=pltpu.CompilerParams(vmem_limit_bytes=8 << 20),
        name="stats",
    )(activations)
    stats = lax.all_to_all(stats, "frame", split_axis=0, concat_axis=0, tiled=True)
    above = lax.ppermute(tail, "frame", [(i, i + 1) for i in range(devices - 1)])
    below = lax.ppermute(head, "frame", [(i + 1, i) for i in range(devices - 1)])
    lines = [
        v.reshape(1, -1)
        for v in (norm_gain, norm_bias, conv_bias, down_bias, time_bias, head_bias)
    ]
    pairs = cols // 2
    prepared = pl.pallas_call(
        functools.partial(prep_kernel, pairs=pairs),
        out_shape=(
            jax.ShapeDtypeStruct((8, rows // 2 * pairs), jnp.int32),
            jax.ShapeDtypeStruct((shards, channels), BF16),
            jax.ShapeDtypeStruct((8, channels), F32),
            jax.ShapeDtypeStruct((3 * channels, channels), BF16),
        ),
        in_specs=[pl.BlockSpec(memory_space=pltpu.SMEM), *vmem(10)],
        out_specs=tuple(vmem(4)),
        compiler_params=pltpu.CompilerParams(vmem_limit_bytes=4 << 20),
        cost_estimate=pl.CostEstimate(flops=20_000_000_000, bytes_accessed=0, transcendentals=0),
        name="prep",
    )(position, tile_shard.transpose(1, 0, 2), tile_slot.transpose(1, 0, 2), *lines, head_weight.T, time_weight)
    weights = (conv_weight, down_weight)
    outgoing = pl.pallas_call(
        encode_kernel,
        out_shape=jax.ShapeDtypeStruct((shards * PACK, channels), BF16),
        in_specs=[
            pl.BlockSpec(memory_space=pltpu.SMEM),
            *vmem(10),
        ],
        out_specs=pl.BlockSpec(memory_space=pltpu.VMEM),
        scratch_shapes=[
            pltpu.VMEM((frames, rows + 3, cols, channels), F32),
            pltpu.VMEM((frames, rows + 3, cols // 2, 4 * channels), BF16),
            pltpu.VMEM((frames, rows + 1, cols // 2, 3 * channels), BF16),
            pltpu.VMEM((frames, rows // 2 * (cols // 2), channels), BF16),
        ],
        compiler_params=pltpu.CompilerParams(vmem_limit_bytes=32 << 20),
        name="encode",
    )(
        position, activations, above, below, stats, prepared[2], prepared[3], *prepared[:2], *weights
    )
    arrived = lax.all_to_all(
        outgoing.reshape(shards, PACK, channels), "clip", split_axis=0, concat_axis=0, tiled=True
    )
    packed = pl.pallas_call(
        place_kernel,
        out_shape=jax.ShapeDtypeStruct((lats * 2 * shards, channels), BF16),
        in_specs=vmem(1),
        out_specs=pl.BlockSpec(memory_space=pltpu.VMEM),
        compiler_params=pltpu.CompilerParams(vmem_limit_bytes=8 << 20),
        name="place",
    )(arrived.reshape(shards * PACK, channels))
    return packed.reshape(lats, 2 * shards, channels)


def solution(mesh):
    placed = (
        P("clip", None, "frame", None, None),
        P(),
        P(),
        P(),
        P(),
        P(),
        P(),
        P(),
        P(),
        P(),
        P(),
        P("clip", None, "frame"),
        P("clip", None, "frame"),
    )
    return jax.shard_map(
        local,
        mesh=mesh,
        in_specs=placed,
        out_specs=P(None, ("clip", "frame"), None),
        check_vma=False,
    )
```

```python
import functools

import jax
import jax.numpy as jnp
from jax import lax
from jax.experimental import pallas as pl
from jax.experimental.pallas import tpu as pltpu
from jax.sharding import PartitionSpec as P

GROUPS = 32
EPSILON = 1e-06
PACK = 8
F32 = jnp.float32
BF16 = jnp.bfloat16


def iota(shape, dim):
    return lax.broadcasted_iota(jnp.int32, shape, dim)


def onehot(mask):
    return jnp.where(mask, 1.0, 0.0).astype(BF16)


def matmul(lhs, rhs):
    return jnp.dot(lhs, rhs, preferred_element_type=F32)


def matmul_nt(lhs, rhs):
    return lax.dot_general(lhs, rhs, (((1,), (1,)), ((), ())), preferred_element_type=F32)


def stats_kernel(x_ref, stats_ref, tail_ref, head_ref):
    frames, rows, cols, channels = x_ref.shape
    count = frames * rows * cols

    def over_all(change):
        parts = [jnp.sum(change(x_ref[f].astype(F32)), axis=0) for f in range(frames)]
        return jnp.sum(sum(parts), axis=0, keepdims=True)

    total = over_all(lambda v: v)
    mean = total / count
    spread = over_all(lambda v: (v - mean) * (v - mean))
    both = jnp.concatenate([total, spread], axis=0)
    for d in range(stats_ref.shape[0]):
        stats_ref[d] = both
    tail_ref[...] = x_ref[:, rows - 1 :]
    head_ref[...] = x_ref[:, :2]


def over_group(values, width):
    lane = iota(values.shape, 1)
    size = values.shape[1]
    step = 1
    while step < width:
        after = pltpu.roll(values, size - step, 1)
        before = pltpu.roll(values, step, 1)
        values = values + jnp.where((lane // step) % 2 == 0, after, before)
        step *= 2
    return values


def encode_kernel(
    pos_ref, x_ref, up_ref, dn_ref, stats_ref, vec_ref, head_ref, keys_ref, slots_ref, cw_ref,
    dw_ref, tw_ref, out_ref, raw, hid, skip, red,
):
    frames, rows, cols, channels = x_ref.shape
    pairs = cols // 2
    devices = stats_ref.shape[0]
    per_group = channels // GROUPS
    count = frames * rows * cols
    lats = (frames + 1) // 2
    ext = rows + 3
    made = rows + 1

    stats = stats_ref[...]
    sums, devs = stats[:, 0], stats[:, 1]
    entries = count * devices * per_group
    mean = over_group(jnp.broadcast_to(jnp.sum(sums, axis=0, keepdims=True), (8, channels)), per_group)
    mean = mean[:1] / entries
    off = sums / count - mean
    var = jnp.sum(devs + count * (off * off), axis=0, keepdims=True)
    var = over_group(jnp.broadcast_to(var, (8, channels)), per_group)[:1] / entries
    scale = lax.rsqrt(var + EPSILON) * vec_ref[0:1] * 0.5
    shift = vec_ref[1:2] * 0.5

    place = pos_ref[0]
    has_up = jnp.where(place > 0, 1.0, 0.0).astype(F32)
    has_dn = jnp.where(place < devices - 1, 1.0, 0.0).astype(F32)

    def row(f, r):
        if r == 0:
            return up_ref[f, 0]
        if r <= rows:
            return x_ref[f, r - 1]
        return dn_ref[f, r - 1 - rows]

    pair_id = iota((pairs, channels), 0)
    conv_bias = vec_ref[2:3]
    for f in range(frames):
        for r in range(ext):
            raw[f, r] = row(f, r).astype(F32)
            halves = []
            for parity in range(2):
                half = (raw[f, r, pl.ds(parity, pairs, stride=2), :] - mean) * scale + shift
                half = half + half * jnp.tanh(half)
                if r == 0:
                    half = half * has_up
                elif r > rows:
                    half = half * has_dn
                halves.append(half)
            even, odd = halves
            left = jnp.where(pair_id == 0, 0.0, pltpu.roll(odd, 1, 0))
            right = jnp.where(pair_id == pairs - 1, 0.0, pltpu.roll(even, pairs - 1, 0))
            for u, part in enumerate((left, even, odd, right)):
                hid[f, r, :, u * channels : (u + 1) * channels] = part.astype(BF16)

    none = jnp.zeros((channels, channels), BF16)

    def pair_weight(a, b):
        w = [cw_ref[a, b, e] for e in range(3)]
        return jnp.concatenate(
            [
                jnp.concatenate([w[0], w[1], w[2], none], axis=0),
                jnp.concatenate([none, w[0], w[1], w[2]], axis=0),
            ],
            axis=1,
        )

    for f in range(frames):
        acc = jnp.zeros((made * pairs, 2 * channels), F32)
        for a in range(3):
            g = f - 2 + a
            if g < 0:
                continue
            for b in range(3):
                lhs = hid[g, b : b + made].reshape(made * pairs, 4 * channels)
                acc = acc + matmul(lhs, pair_weight(a, b))
        for r in range(made):
            block = acc[r * pairs : (r + 1) * pairs]
            ends = []
            for parity in range(2):
                half = block[:, parity * channels : (parity + 1) * channels] + conv_bias
                half = half + raw[f, r + 1, pl.ds(parity, pairs, stride=2), :]
                if r == rows:
                    half = half * has_dn
                ends.append(half)
            right = jnp.where(pair_id == pairs - 1, 0.0, pltpu.roll(ends[0], pairs - 1, 0))
            for u, part in enumerate((*ends, right)):
                skip[f, r, :, u * channels : (u + 1) * channels] = part.astype(BF16)

    down = jnp.concatenate([dw_ref[b, e] for b in range(3) for e in range(3)], axis=0)
    spots = rows // 2 * pairs
    for f in range(frames):
        lhs = jnp.concatenate(
            [
                jnp.concatenate([skip[f, 2 * i + b] for i in range(rows // 2)], axis=0)
                for b in range(3)
            ],
            axis=1,
        )
        red[f] = (matmul(lhs, down) + vec_ref[3:4]).astype(BF16)

    blank = jnp.zeros((spots, channels), BF16)
    taps = jnp.concatenate(
        [
            jnp.concatenate(
                [red[2 * l - 2 + k] if 2 * l - 2 + k >= 0 else blank for k in range(3)], axis=1
            )
            for l in range(lats)
        ],
        axis=0,
    )
    mixing = jnp.concatenate([tw_ref[k] for k in range(3)], axis=0)
    mixed = (matmul(taps, mixing) + vec_ref[4:5]).astype(BF16)
    width = channels // 4
    latent = matmul_nt(mixed, head_ref[...]) + vec_ref[5:6]
    spot = iota(latent.shape, 0) % spots
    corner = (spot // pairs) % 2 * 2 + spot % 2
    latent = jnp.where(iota(latent.shape, 1) // width == corner, latent, 0.0).astype(BF16)

    line = iota((out_ref.shape[0], spots), 0)
    chosen = [onehot(line == keys_ref[l : l + 1]) for l in range(lats)]
    out = matmul(jnp.concatenate(chosen, axis=1), latent)
    out_ref[...] = (out + put_slots(slots_ref[...], out_ref.shape[0])).astype(BF16)


def put_slots(slots, lines):
    line = iota((lines, slots.shape[0]), 0)
    put = onehot((line % PACK == PACK - 2) & (line // PACK == iota(line.shape, 1)))
    return matmul(put, slots)


def prep_kernel(*refs, pairs):
    pos_ref, shard_ref, slot_ref, *line_refs, hw_ref = refs[:-4]
    keys_ref, slots_ref, vec_ref, head_ref = refs[-4:]
    copies = vec_ref.shape[1] // hw_ref.shape[0]
    for i, ref in enumerate(line_refs):
        row = ref[...]
        if row.shape[1] < vec_ref.shape[1]:
            row = jnp.concatenate([row] * copies, axis=1)
        vec_ref[i : i + 1] = row
    vec_ref[len(line_refs) :] = jnp.zeros((8 - len(line_refs), vec_ref.shape[1]), F32)
    head_ref[...] = jnp.concatenate([hw_ref[...]] * copies, axis=0)
    lats, _, tiles = shard_ref.shape
    shards, channels = slots_ref.shape
    spots = keys_ref.shape[1]
    slot_base = pos_ref[0] * (2 * shards)
    upper = onehot(iota((tiles, tiles), 0) < iota((tiles, tiles), 1))
    at = iota((tiles, spots), 1)
    grown = at // (2 * pairs) * (pairs // 2) + at % pairs // 2
    grown = onehot(grown == iota((tiles, spots), 0))
    slots = jnp.zeros((shards, channels), F32)
    keys = []
    for l in range(lats):
        shard = jnp.broadcast_to(shard_ref[l], (shards, tiles))
        mine = shard == iota((shards, tiles), 0)
        earlier = matmul(onehot(mine), upper)
        rank = jnp.sum(jnp.where(mine, earlier, 0.0), axis=0, keepdims=True)
        keys.append(shard_ref[l].astype(F32) * PACK + 2 * l + rank)
        number = jnp.broadcast_to(slot_ref[l] - slot_base + 1, (shards, tiles))
        number = jnp.where(mine, number.astype(F32), 0.0).astype(BF16)
        which = jnp.broadcast_to(rank.astype(jnp.int32) + 2 * l, (channels, tiles))
        slots = slots + matmul_nt(number, onehot(which == iota((channels, tiles), 0) % PACK))
    keys = jnp.concatenate(keys + [jnp.zeros((8 - lats, tiles), F32)], axis=0)
    keys_ref[...] = matmul(keys.astype(BF16), grown).astype(jnp.int32)
    slots_ref[...] = slots.astype(BF16)


def place_kernel(got_ref, out_ref):
    lines, width = got_ref.shape
    slots = out_ref.shape[0]
    shards = lines // PACK
    got = got_ref[...]
    pick = iota((shards, lines), 1) == iota((shards, lines), 0) * PACK + PACK - 2
    table = matmul(onehot(pick), got)
    table = jnp.concatenate([table] * (lines // width), axis=1)
    table = jnp.where(iota(table.shape, 1) // PACK == iota(table.shape, 0), table, 0.0)
    slot = jnp.sum(table, axis=0, keepdims=True).astype(jnp.int32)
    own = iota((1, lines), 1) % PACK
    per_lat = slots // ((PACK - 2) // 2)
    want = jnp.where((slot > 0) & (own < PACK - 2), slot - 1 + own // 2 * per_lat, -1)
    out_ref[...] = matmul(onehot(iota((slots, lines), 0) == want), got).astype(BF16)


def vmem(count):
    return [pl.BlockSpec(memory_space=pltpu.VMEM)] * count


def local(
    inputs,
    norm_gain,
    norm_bias,
    conv_weight,
    conv_bias,
    down_weight,
    down_bias,
    time_weight,
    time_bias,
    head_weight,
    head_bias,
    tile_shard,
    tile_slot,
):
    activations = inputs[0]
    frames, rows, cols, channels = activations.shape
    devices = lax.axis_size("frame")
    shards = lax.axis_size("clip")
    lats = (frames + 1) // 2
    position = lax.axis_index("frame").astype(jnp.int32).reshape(1)

    stats, tail, head = pl.pallas_call(
        stats_kernel,
        out_shape=(
            jax.ShapeDtypeStruct((devices, 2, channels), F32),
            jax.ShapeDtypeStruct((frames, 1, cols, channels), BF16),
            jax.ShapeDtypeStruct((frames, 2, cols, channels), BF16),
        ),
        in_specs=vmem(1),
        out_specs=tuple(vmem(3)),
        compiler_params=pltpu.CompilerParams(vmem_limit_bytes=8 << 20),
        name="stats",
    )(activations)
    stats = lax.all_to_all(stats, "frame", split_axis=0, concat_axis=0, tiled=True)
    above = lax.ppermute(tail, "frame", [(i, i + 1) for i in range(devices - 1)])
    below = lax.ppermute(head, "frame", [(i + 1, i) for i in range(devices - 1)])
    lines = [
        v.reshape(1, -1)
        for v in (norm_gain, norm_bias, conv_bias, down_bias, time_bias, head_bias)
    ]
    pairs = cols // 2
    prepared = pl.pallas_call(
        functools.partial(prep_kernel, pairs=pairs),
        out_shape=(
            jax.ShapeDtypeStruct((8, rows // 2 * pairs), jnp.int32),
            jax.ShapeDtypeStruct((shards, channels), BF16),
            jax.ShapeDtypeStruct((8, channels), F32),
            jax.ShapeDtypeStruct((channels, channels), BF16),
        ),
        in_specs=[pl.BlockSpec(memory_space=pltpu.SMEM), *vmem(9)],
        out_specs=tuple(vmem(4)),
        compiler_params=pltpu.CompilerParams(vmem_limit_bytes=4 << 20),
        cost_estimate=pl.CostEstimate(flops=20_000_000_000, bytes_accessed=0, transcendentals=0),
        name="prep",
    )(position, tile_shard.transpose(1, 0, 2), tile_slot.transpose(1, 0, 2), *lines, head_weight.T)
    weights = (conv_weight, down_weight, time_weight)
    outgoing = pl.pallas_call(
        encode_kernel,
        out_shape=jax.ShapeDtypeStruct((shards * PACK, channels), BF16),
        in_specs=[
            pl.BlockSpec(memory_space=pltpu.SMEM),
            *vmem(11),
        ],
        out_specs=pl.BlockSpec(memory_space=pltpu.VMEM),
        scratch_shapes=[
            pltpu.VMEM((frames, rows + 3, cols, channels), F32),
            pltpu.VMEM((frames, rows + 3, cols // 2, 4 * channels), BF16),
            pltpu.VMEM((frames, rows + 1, cols // 2, 3 * channels), BF16),
            pltpu.VMEM((frames, rows // 2 * (cols // 2), channels), BF16),
        ],
        compiler_params=pltpu.CompilerParams(vmem_limit_bytes=32 << 20),
        name="encode",
    )(
        position, activations, above, below, stats, prepared[2], prepared[3], *prepared[:2], *weights
    )
    arrived = lax.all_to_all(
        outgoing.reshape(shards, PACK, channels), "clip", split_axis=0, concat_axis=0, tiled=True
    )
    packed = pl.pallas_call(
        place_kernel,
        out_shape=jax.ShapeDtypeStruct((lats * 2 * shards, channels), BF16),
        in_specs=vmem(1),
        out_specs=pl.BlockSpec(memory_space=pltpu.VMEM),
        compiler_params=pltpu.CompilerParams(vmem_limit_bytes=8 << 20),
        name="place",
    )(arrived.reshape(shards * PACK, channels))
    return packed.reshape(lats, 2 * shards, channels)


def solution(mesh):
    placed = (
        P("clip", None, "frame", None, None),
        P(),
        P(),
        P(),
        P(),
        P(),
        P(),
        P(),
        P(),
        P(),
        P(),
        P("clip", None, "frame"),
        P("clip", None, "frame"),
    )
    return jax.shard_map(
        local,
        mesh=mesh,
        in_specs=placed,
        out_specs=P(None, ("clip", "frame"), None),
        check_vma=False,
    )
```

```python
import functools

import jax
import jax.numpy as jnp
from jax import lax
from jax.experimental import pallas as pl
from jax.experimental.pallas import tpu as pltpu
from jax.sharding import PartitionSpec as P

GROUPS = 32
EPSILON = 1e-06
PACK = 8
F32 = jnp.float32
BF16 = jnp.bfloat16


def iota(shape, dim):
    return lax.broadcasted_iota(jnp.int32, shape, dim)


def onehot(mask):
    return jnp.where(mask, 1.0, 0.0).astype(BF16)


def matmul(lhs, rhs):
    return jnp.dot(lhs, rhs, preferred_element_type=F32)


def matmul_nt(lhs, rhs):
    return lax.dot_general(lhs, rhs, (((1,), (1,)), ((), ())), preferred_element_type=F32)


def stats_kernel(x_ref, stats_ref, tail_ref, head_ref, held, sems):
    frames, rows, cols, channels = x_ref.shape
    count = rows * cols
    copies = [pltpu.make_async_copy(x_ref.at[f], held.at[f], sems.at[f]) for f in range(frames)]
    for copy in copies:
        copy.start()
    totals, spreads = [], []
    for f in range(frames):
        copies[f].wait()
        block = held[f].astype(F32)
        total = jnp.sum(jnp.sum(block, axis=0), axis=0, keepdims=True)
        off = block - total / count
        totals.append(total)
        spreads.append(jnp.sum(off * off, axis=0))
        tail_ref[f] = held[f, rows - 1 :]
        head_ref[f] = held[f, :2]
    total = sum(totals)
    mean = total / (count * frames)
    spread = jnp.sum(sum(spreads), axis=0, keepdims=True)
    for f in range(frames):
        off = totals[f] / count - mean
        spread = spread + count * (off * off)
    both = jnp.concatenate([total, spread], axis=0)
    for d in range(stats_ref.shape[0]):
        stats_ref[d] = both


def over_group(values, width):
    lane = iota(values.shape, 1)
    size = values.shape[1]
    step = 1
    while step < width:
        after = pltpu.roll(values, size - step, 1)
        before = pltpu.roll(values, step, 1)
        values = values + jnp.where((lane // step) % 2 == 0, after, before)
        step *= 2
    return values


def encode_kernel(
    pos_ref, x_ref, up_ref, dn_ref, stats_ref, vec_ref, head_ref, keys_ref, slots_ref, cw_ref,
    dw_ref, tw_ref, out_ref, raw, hid, skip, red,
):
    frames, rows, cols, channels = x_ref.shape
    pairs = cols // 2
    devices = stats_ref.shape[0]
    per_group = channels // GROUPS
    count = frames * rows * cols
    lats = (frames + 1) // 2
    ext = rows + 3
    made = rows + 1

    stats = stats_ref[...]
    sums, devs = stats[:, 0], stats[:, 1]
    entries = count * devices * per_group
    mean = over_group(jnp.broadcast_to(jnp.sum(sums, axis=0, keepdims=True), (8, channels)), per_group)
    mean = mean[:1] / entries
    off = sums / count - mean
    var = jnp.sum(devs + count * (off * off), axis=0, keepdims=True)
    var = over_group(jnp.broadcast_to(var, (8, channels)), per_group)[:1] / entries
    scale = lax.rsqrt(var + EPSILON) * vec_ref[0:1] * 0.5
    shift = vec_ref[1:2] * 0.5

    place = pos_ref[0]
    has_up = jnp.where(place > 0, 1.0, 0.0).astype(F32)
    has_dn = jnp.where(place < devices - 1, 1.0, 0.0).astype(F32)

    def row(f, r):
        if r == 0:
            return up_ref[f, 0]
        if r <= rows:
            return x_ref[f, r - 1]
        return dn_ref[f, r - 1 - rows]

    pair_id = iota((pairs, channels), 0)
    conv_bias = vec_ref[2:3]
    for f in range(frames):
        for r in range(ext):
            raw[f, r] = row(f, r).astype(F32)
            halves = []
            for parity in range(2):
                half = (raw[f, r, pl.ds(parity, pairs, stride=2), :] - mean) * scale + shift
                half = half + half * jnp.tanh(half)
                if r == 0:
                    half = half * has_up
                elif r > rows:
                    half = half * has_dn
                halves.append(half)
            even, odd = halves
            left = jnp.where(pair_id == 0, 0.0, pltpu.roll(odd, 1, 0))
            right = jnp.where(pair_id == pairs - 1, 0.0, pltpu.roll(even, pairs - 1, 0))
            for u, part in enumerate((left, even, odd, right)):
                hid[f, r, :, u * channels : (u + 1) * channels] = part.astype(BF16)

    none = jnp.zeros((channels, channels), BF16)

    def pair_weight(a, b):
        w = [cw_ref[a, b, e] for e in range(3)]
        return jnp.concatenate(
            [
                jnp.concatenate([w[0], w[1], w[2], none], axis=0),
                jnp.concatenate([none, w[0], w[1], w[2]], axis=0),
            ],
            axis=1,
        )

    for f in range(frames):
        acc = jnp.zeros((made * pairs, 2 * channels), F32)
        for a in range(3):
            g = f - 2 + a
            if g < 0:
                continue
            for b in range(3):
                lhs = hid[g, b : b + made].reshape(made * pairs, 4 * channels)
                acc = acc + matmul(lhs, pair_weight(a, b))
        for r in range(made):
            block = acc[r * pairs : (r + 1) * pairs]
            ends = []
            for parity in range(2):
                half = block[:, parity * channels : (parity + 1) * channels] + conv_bias
                half = half + raw[f, r + 1, pl.ds(parity, pairs, stride=2), :]
                if r == rows:
                    half = half * has_dn
                ends.append(half)
            right = jnp.where(pair_id == pairs - 1, 0.0, pltpu.roll(ends[0], pairs - 1, 0))
            for u, part in enumerate((*ends, right)):
                skip[f, r, :, u * channels : (u + 1) * channels] = part.astype(BF16)

    down = jnp.concatenate([dw_ref[b, e] for b in range(3) for e in range(3)], axis=0)
    spots = rows // 2 * pairs
    for f in range(frames):
        lhs = jnp.concatenate(
            [
                jnp.concatenate([skip[f, 2 * i + b] for i in range(rows // 2)], axis=0)
                for b in range(3)
            ],
            axis=1,
        )
        red[f] = (matmul(lhs, down) + vec_ref[3:4]).astype(BF16)

    blank = jnp.zeros((spots, channels), BF16)
    taps = jnp.concatenate(
        [
            jnp.concatenate(
                [red[2 * l - 2 + k] if 2 * l - 2 + k >= 0 else blank for k in range(3)], axis=1
            )
            for l in range(lats)
        ],
        axis=0,
    )
    mixing = jnp.concatenate([tw_ref[k] for k in range(3)], axis=0)
    mixed = (matmul(taps, mixing) + vec_ref[4:5]).astype(BF16)
    width = channels // 4
    latent = matmul_nt(mixed, head_ref[...]) + vec_ref[5:6]
    spot = iota(latent.shape, 0) % spots
    corner = (spot // pairs) % 2 * 2 + spot % 2
    latent = jnp.where(iota(latent.shape, 1) // width == corner, latent, 0.0).astype(BF16)

    line = iota((out_ref.shape[0], spots), 0)
    chosen = [onehot(line == keys_ref[l : l + 1]) for l in range(lats)]
    out = matmul(jnp.concatenate(chosen, axis=1), latent)
    out_ref[...] = (out + put_slots(slots_ref[...], out_ref.shape[0])).astype(BF16)


def put_slots(slots, lines):
    line = iota((lines, slots.shape[0]), 0)
    put = onehot((line % PACK == PACK - 2) & (line // PACK == iota(line.shape, 1)))
    return matmul(put, slots)


def prep_kernel(*refs, pairs):
    pos_ref, shard_ref, slot_ref, *line_refs, hw_ref = refs[:-4]
    keys_ref, slots_ref, vec_ref, head_ref = refs[-4:]
    copies = vec_ref.shape[1] // hw_ref.shape[0]
    for i, ref in enumerate(line_refs):
        row = ref[...]
        if row.shape[1] < vec_ref.shape[1]:
            row = jnp.concatenate([row] * copies, axis=1)
        vec_ref[i : i + 1] = row
    vec_ref[len(line_refs) :] = jnp.zeros((8 - len(line_refs), vec_ref.shape[1]), F32)
    head_ref[...] = jnp.concatenate([hw_ref[...]] * copies, axis=0)
    lats, _, tiles = shard_ref.shape
    shards, channels = slots_ref.shape
    spots = keys_ref.shape[1]
    slot_base = pos_ref[0] * (2 * shards)
    upper = onehot(iota((tiles, tiles), 0) < iota((tiles, tiles), 1))
    at = iota((tiles, spots), 1)
    grown = at // (2 * pairs) * (pairs // 2) + at % pairs // 2
    grown = onehot(grown == iota((tiles, spots), 0))
    slots = jnp.zeros((shards, channels), F32)
    keys = []
    for l in range(lats):
        shard = jnp.broadcast_to(shard_ref[l], (shards, tiles))
        mine = shard == iota((shards, tiles), 0)
        earlier = matmul(onehot(mine), upper)
        rank = jnp.sum(jnp.where(mine, earlier, 0.0), axis=0, keepdims=True)
        keys.append(shard_ref[l].astype(F32) * PACK + 2 * l + rank)
        number = jnp.broadcast_to(slot_ref[l] - slot_base + 1, (shards, tiles))
        number = jnp.where(mine, number.astype(F32), 0.0).astype(BF16)
        which = jnp.broadcast_to(rank.astype(jnp.int32) + 2 * l, (channels, tiles))
        slots = slots + matmul_nt(number, onehot(which == iota((channels, tiles), 0) % PACK))
    keys = jnp.concatenate(keys + [jnp.zeros((8 - lats, tiles), F32)], axis=0)
    keys_ref[...] = matmul(keys.astype(BF16), grown).astype(jnp.int32)
    slots_ref[...] = slots.astype(BF16)


def place_kernel(got_ref, out_ref):
    lines, width = got_ref.shape
    slots = out_ref.shape[0]
    shards = lines // PACK
    got = got_ref[...]
    pick = iota((shards, lines), 1) == iota((shards, lines), 0) * PACK + PACK - 2
    table = matmul(onehot(pick), got)
    table = jnp.concatenate([table] * (lines // width), axis=1)
    table = jnp.where(iota(table.shape, 1) // PACK == iota(table.shape, 0), table, 0.0)
    slot = jnp.sum(table, axis=0, keepdims=True).astype(jnp.int32)
    own = iota((1, lines), 1) % PACK
    per_lat = slots // ((PACK - 2) // 2)
    want = jnp.where((slot > 0) & (own < PACK - 2), slot - 1 + own // 2 * per_lat, -1)
    out_ref[...] = matmul(onehot(iota((slots, lines), 0) == want), got).astype(BF16)


def vmem(count):
    return [pl.BlockSpec(memory_space=pltpu.VMEM)] * count


def local(
    inputs,
    norm_gain,
    norm_bias,
    conv_weight,
    conv_bias,
    down_weight,
    down_bias,
    time_weight,
    time_bias,
    head_weight,
    head_bias,
    tile_shard,
    tile_slot,
):
    activations = inputs[0]
    frames, rows, cols, channels = activations.shape
    devices = lax.axis_size("frame")
    shards = lax.axis_size("clip")
    lats = (frames + 1) // 2
    position = lax.axis_index("frame").astype(jnp.int32).reshape(1)

    stats, tail, head = pl.pallas_call(
        stats_kernel,
        out_shape=(
            jax.ShapeDtypeStruct((devices, 2, channels), F32),
            jax.ShapeDtypeStruct((frames, 1, cols, channels), BF16),
            jax.ShapeDtypeStruct((frames, 2, cols, channels), BF16),
        ),
        in_specs=[pl.BlockSpec(memory_space=pltpu.HBM)],
        out_specs=tuple(vmem(3)),
        scratch_shapes=[
            pltpu.VMEM((frames, rows, cols, channels), BF16),
            pltpu.SemaphoreType.DMA((frames,)),
        ],
        compiler_params=pltpu.CompilerParams(vmem_limit_bytes=63 << 20),
        name="stats",
    )(activations)
    stats = lax.all_to_all(stats, "frame", split_axis=0, concat_axis=0, tiled=True)
    above = lax.ppermute(tail, "frame", [(i, i + 1) for i in range(devices - 1)])
    below = lax.ppermute(head, "frame", [(i + 1, i) for i in range(devices - 1)])
    lines = [
        v.reshape(1, -1)
        for v in (norm_gain, norm_bias, conv_bias, down_bias, time_bias, head_bias)
    ]
    pairs = cols // 2
    prepared = pl.pallas_call(
        functools.partial(prep_kernel, pairs=pairs),
        out_shape=(
            jax.ShapeDtypeStruct((8, rows // 2 * pairs), jnp.int32),
            jax.ShapeDtypeStruct((shards, channels), BF16),
            jax.ShapeDtypeStruct((8, channels), F32),
            jax.ShapeDtypeStruct((channels, channels), BF16),
        ),
        in_specs=[pl.BlockSpec(memory_space=pltpu.SMEM), *vmem(9)],
        out_specs=tuple(vmem(4)),
        compiler_params=pltpu.CompilerParams(vmem_limit_bytes=4 << 20),
        cost_estimate=pl.CostEstimate(flops=20_000_000_000, bytes_accessed=0, transcendentals=0),
        name="prep",
    )(position, tile_shard.transpose(1, 0, 2), tile_slot.transpose(1, 0, 2), *lines, head_weight.T)
    weights = (conv_weight, down_weight, time_weight)
    outgoing = pl.pallas_call(
        encode_kernel,
        out_shape=jax.ShapeDtypeStruct((shards * PACK, channels), BF16),
        in_specs=[
            pl.BlockSpec(memory_space=pltpu.SMEM),
            *vmem(11),
        ],
        out_specs=pl.BlockSpec(memory_space=pltpu.VMEM),
        scratch_shapes=[
            pltpu.VMEM((frames, rows + 3, cols, channels), F32),
            pltpu.VMEM((frames, rows + 3, cols // 2, 4 * channels), BF16),
            pltpu.VMEM((frames, rows + 1, cols // 2, 3 * channels), BF16),
            pltpu.VMEM((frames, rows // 2 * (cols // 2), channels), BF16),
        ],
        compiler_params=pltpu.CompilerParams(vmem_limit_bytes=32 << 20),
        name="encode",
    )(
        position, activations, above, below, stats, prepared[2], prepared[3], *prepared[:2], *weights
    )
    arrived = lax.all_to_all(
        outgoing.reshape(shards, PACK, channels), "clip", split_axis=0, concat_axis=0, tiled=True
    )
    packed = pl.pallas_call(
        place_kernel,
        out_shape=jax.ShapeDtypeStruct((lats * 2 * shards, channels), BF16),
        in_specs=vmem(1),
        out_specs=pl.BlockSpec(memory_space=pltpu.VMEM),
        compiler_params=pltpu.CompilerParams(vmem_limit_bytes=8 << 20),
        name="place",
    )(arrived.reshape(shards * PACK, channels))
    return packed.reshape(lats, 2 * shards, channels)


def solution(mesh):
    placed = (
        P("clip", None, "frame", None, None),
        P(),
        P(),
        P(),
        P(),
        P(),
        P(),
        P(),
        P(),
        P(),
        P(),
        P("clip", None, "frame"),
        P("clip", None, "frame"),
    )
    return jax.shard_map(
        local,
        mesh=mesh,
        in_specs=placed,
        out_specs=P(None, ("clip", "frame"), None),
        check_vma=False,
    )
```
